32 devices in a mesh: groups: 2 (over y), node: 4 (over z), tp: 4 (over x, core).
Axes of the slice: x: 2, y: 2, z: 4, core: 2. Of those that a mesh axis runs over, the one named last changes fastest.
Arguments:
- queries: bfloat16 [16, 256, 8192], P(('groups', 'node'), None, 'tp'), parts along dimension 0, may hold values from -72 to 72
- new_kv: bfloat16 [2, 16, 256, 1024], P(None, ('groups', 'node'), None, 'tp'), parts along dimension 1, may hold values from -6 to 6
- page_pool: bfloat16 [2, 256, 128, 1024], P(None, ('groups', 'node'), None, 'tp'), parts along dimension 1, may hold values from -6 to 6
- slot_request: int32 [16], P('groups'), parts along dimension 0, may hold values from 0 to 7, as said below
- prefix_len: int32 [16], P('groups'), parts along dimension 0, may hold values from 1 to 2048, as said below
- page_holder: int32 [16, 16], P('groups'), parts along dimension 0, may hold values from 0 to 3, as said below
- page_slot: int32 [16, 16], P('groups'), parts along dimension 0, may hold values from 0 to 31, as said below
- decode_slot: int32 [16], P('groups'), parts along dimension 0, may hold values from 0 to 7, as said below
Outputs:
- attended: bfloat16 [16, 256, 8192], P(('groups', 'node'), None, 'tp'), parts along dimension 0
- decode_kv: bfloat16 [2, 16, 256, 1024], P(None, ('groups', 'node'), None, 'tp'), parts along dimension 1
The draws below stay inside these ranges and needn't reach their ends.
There are 2 independent parts, one for each index of `groups`. The reference program is written for one: setup_inputs(seed, part) draws one part's arguments, and reference() takes and returns one part's arrays. A program takes and returns all parts, laid end to end along the dimension named above; each array names one. Nothing has to cross between parts.
Inputs may be any that keep to these rules, and one draw needn't show every extreme that they name: `slot_request`: a permutation: each request stands in one prefill slot. `prefix_len`: the requests of some prefill node all have 16 * 128 prefix tokens. `page_holder`: entries j < ceil(prefix_len / 128) are used, the others arbitrary; one holder holds at most 8 used pages of the requests of one prefill node, and exactly 8 for some holder and node. `page_slot`: used pages of one holder lie in different slots; unused entries arbitrary. `decode_slot`: a permutation; slot s lies on decode node s // 2; two requests of one prefill node never share a decode node.
All inputs are finite; a program needn't handle non-finite values.
Results may differ from the reference program's by a relative error of at most 0.0032.
Values may be sent and summed in bfloat16 or wider, within the bound.
No kernel may reach another device: no remote copies, remote signals or barrier semaphores. Data moves between devices by JAX's collectives and lax.ppermute only.
A program may use at most 64 MiB of HBM per device.

```python
import jax
import jax.numpy as jnp
from jax import lax

HQ = 64
KVH = 8
HD = 128
PAGE = 128
SUF = 256
MAXP = 16
REQ_DEV = 2
REQS = 8
CAP = 8
SLOTS = 32
N_NODE = 4


def layout(key):
    streams = jax.random.split(jax.random.fold_in(key, 5), 10)
    slot_owner = jax.random.permutation(streams[0], REQS).astype(jnp.int32)
    tokens = jax.random.randint(streams[1], (REQS,), 1, MAXP * PAGE + 1)
    full_node = jax.random.randint(streams[2], (), 0, N_NODE)
    home_node = jnp.arange(REQS, dtype=jnp.int32) // REQ_DEV
    tokens = jnp.where(home_node == full_node, MAXP * PAGE, tokens)
    page_total = (tokens + PAGE - 1) // PAGE
    block_span = REQ_DEV * MAXP
    usable = (jnp.arange(MAXP, dtype=jnp.int32)[None, :] < page_total[:, None]).reshape(N_NODE, block_span).astype(jnp.int32)
    arrival = jnp.cumsum(usable, axis=1) - usable
    cycles = jax.vmap(lambda subkey: jax.random.permutation(subkey, N_NODE))(jax.random.split(streams[3], N_NODE)).astype(jnp.int32)
    holder = jnp.take_along_axis(cycles, arrival % N_NODE, axis=1)
    page_depth = jnp.minimum(arrival // N_NODE, CAP - 1)
    layouts = jax.vmap(lambda subkey: jax.random.permutation(subkey, SLOTS))(jax.random.split(streams[4], N_NODE)).astype(jnp.int32)
    pool_slot = layouts[holder, jnp.arange(N_NODE, dtype=jnp.int32)[:, None] * CAP + page_depth]
    holder = jnp.where(usable == 1, holder, jax.random.randint(streams[5], (N_NODE, block_span), 0, N_NODE))
    pool_slot = jnp.where(usable == 1, pool_slot, jax.random.randint(streams[6], (N_NODE, block_span), 0, SLOTS))
    shifts = jax.random.permutation(streams[7], N_NODE)[:REQ_DEV].astype(jnp.int32)
    base_order = jax.random.permutation(streams[8], N_NODE).astype(jnp.int32)
    member = jnp.arange(REQS, dtype=jnp.int32) % REQ_DEV
    decode_node = base_order[(home_node + shifts[member]) % N_NODE]
    offset = jax.random.randint(streams[9], (N_NODE,), 0, REQ_DEV)
    decode_global = decode_node * REQ_DEV + (member + offset[decode_node]) % REQ_DEV

    def by_request(values):
        return jnp.zeros_like(values).at[slot_owner].set(values)
    return (slot_owner, by_request(tokens.astype(jnp.int32)), by_request(holder.reshape(REQS, MAXP).astype(jnp.int32)), by_request(pool_slot.reshape(REQS, MAXP).astype(jnp.int32)), by_request(decode_global.astype(jnp.int32)))


def normal_pair(key, scale, bound):
    query_key, pair_key = jax.random.split(jax.random.fold_in(key, 21))
    query_part = jnp.clip(scale * jax.random.normal(query_key, (REQS, SUF, HQ * HD), jnp.float32), -bound, bound)
    pair_part = jnp.clip(scale * jax.random.normal(pair_key, (2, REQS, SUF, KVH * HD), jnp.float32), -bound, bound)
    return (query_part, pair_part)


def draw_queries(key, part):
    query_part, pair_part = normal_pair(key, 1.5, 6.0)
    return query_part.astype(jnp.bfloat16)


def draw_new_kv(key, part):
    query_part, pair_part = normal_pair(key, 1.5, 6.0)
    return pair_part.astype(jnp.bfloat16)


def draw_slot_request(key, part):
    return layout(key)[0]


def draw_prefix_len(key, part):
    return layout(key)[1]


def draw_page_holder(key, part):
    return layout(key)[2]


def draw_page_slot(key, part):
    return layout(key)[3]


def draw_decode_slot(key, part):
    return layout(key)[4]


def level_of(rng, shape, pieces, low, largest):
    def one(dim, parts):
        steps = jax.random.uniform(jax.random.fold_in(jax.random.fold_in(rng, 6), dim), (parts,), jnp.float32, low / len(pieces), largest / len(pieces))
        return jnp.repeat(jnp.exp(steps), shape[dim] // parts).reshape((-1,) + (1,) * (len(shape) - dim - 1))

    loudness = one(*pieces[0])
    for cut in pieces[1:]:
        loudness = loudness * one(*cut)
    return loudness


def scatter_about(own_key, extent, spread, most, cuts=(), kind=jnp.bfloat16):
    drawn = jax.random.normal(own_key, extent, jnp.float32) * spread
    if len(cuts) > 0:
        drawn = level_of(own_key, extent, cuts, -0.22, 0.18) * drawn
    return jnp.clip(drawn, min=-most, max=most).astype(kind)


def setup_inputs(seed: int = 0, part: int = 0) -> dict:
    seeds = jax.random.split(jax.random.key(seed), 9)
    part_keys = jax.random.split(jax.random.fold_in(seeds[8], part), 9)
    return {
        "queries": draw_queries(jax.random.fold_in(jax.random.fold_in(seeds[8], part), 71), part),
        "new_kv": draw_new_kv(jax.random.fold_in(jax.random.fold_in(seeds[8], part), 71), part),
        "page_pool": scatter_about(part_keys[2], (2, N_NODE * SLOTS, PAGE, KVH * HD), 1.5, 6.0, ((1, 4), (3, 4))),
        "slot_request": draw_slot_request(jax.random.fold_in(jax.random.fold_in(seeds[8], part), 71), part),
        "prefix_len": draw_prefix_len(jax.random.fold_in(jax.random.fold_in(seeds[8], part), 71), part),
        "page_holder": draw_page_holder(jax.random.fold_in(jax.random.fold_in(seeds[8], part), 71), part),
        "page_slot": draw_page_slot(jax.random.fold_in(jax.random.fold_in(seeds[8], part), 71), part),
        "decode_slot": draw_decode_slot(jax.random.fold_in(jax.random.fold_in(seeds[8], part), 71), part),
    }


def attend_group(query_rows, key_rows, value_rows, prefix_tokens):
    suffix, group_size, head_width = query_rows.shape
    prefix_span = key_rows.shape[0] - suffix
    step_len = min(suffix, max(1, 512 // group_size))
    key_index = jnp.arange(key_rows.shape[0], dtype=jnp.int32)
    softmax_scale = head_width ** -0.5

    def one_block(first_row):
        query_block = lax.dynamic_slice_in_dim(query_rows, first_row, step_len, 0).reshape(step_len * group_size, head_width)
        scores = jnp.einsum("rd,kd->rk", query_block, key_rows, preferred_element_type=jnp.float32) * softmax_scale
        position = first_row + jnp.arange(step_len * group_size, dtype=jnp.int32) // group_size
        visible = jnp.where(key_index[None, :] < prefix_span, key_index[None, :] < prefix_tokens, key_index[None, :] - prefix_span <= position[:, None])
        scores = jnp.where(visible, scores, -jnp.inf)
        row_max = jnp.max(scores, axis=1, keepdims=True)
        weights = jnp.exp(scores - row_max)
        row_total = jnp.sum(weights, axis=1, keepdims=True)
        product = jnp.dot(weights.astype(jnp.bfloat16), value_rows, preferred_element_type=jnp.float32)
        return (product / row_total).astype(jnp.bfloat16).reshape(step_len, group_size, head_width)

    block_starts = jnp.arange(suffix // step_len, dtype=jnp.int32) * step_len
    return lax.map(one_block, block_starts).reshape(suffix, group_size, head_width)


def reference(queries, new_kv, page_pool, slot_request, prefix_len, page_holder, page_slot, decode_slot):
    per_group = HQ // KVH

    def per_slot(slot_index):
        request = slot_request[slot_index]
        pool_rows = page_holder[request] * SLOTS + page_slot[request]
        cached_pages = jnp.take(page_pool, pool_rows, axis=1).reshape(2, MAXP * PAGE, KVH * HD)
        fresh_pages = lax.dynamic_index_in_dim(new_kv, slot_index, 1, keepdims=False)
        joined = jnp.concatenate([cached_pages, fresh_pages], axis=1)
        query_heads = lax.dynamic_index_in_dim(queries, slot_index, 0, keepdims=False).reshape(SUF, KVH, per_group, HD)
        outputs = []
        for kv_head in range(KVH):
            outputs.append(attend_group(query_heads[:, kv_head], joined[0, :, kv_head * HD:(kv_head + 1) * HD], joined[1, :, kv_head * HD:(kv_head + 1) * HD], prefix_len[request]))
        return jnp.stack(outputs, axis=1).reshape(SUF, HQ * HD)

    attended = lax.map(per_slot, jnp.arange(REQS, dtype=jnp.int32))
    target = jnp.take(decode_slot, slot_request)
    decode_kv = jnp.zeros(new_kv.shape, new_kv.dtype).at[:, target].set(new_kv)
    return attended, decode_kv
```

```python
import functools
import math

import jax
import jax.numpy as jnp
from jax import lax
from jax.experimental import pallas as pl
from jax.experimental.pallas import tpu as pltpu
from jax.sharding import PartitionSpec as P

HD = 128
BLOCK_PAGES = 4
MASKED = -1e30
ANY = pl.BlockSpec(memory_space=pl.ANY)
VMEM = pl.BlockSpec(memory_space=pltpu.VMEM)


def message_plan(nodes, capacity):
    half = nodes // 2
    others = [k for k in range(1, nodes) if k != half]
    cut = (capacity + 1) // 2
    stages = [[(half, 0, capacity)]] if nodes > 1 else []
    if others:
        stages.append([(k, 0, cut) for k in others])
        if cut < capacity:
            stages.append([(k, cut, capacity) for k in others])
    return stages


def pages_of(prefix_len_ref, request, page_len):
    return lax.div(prefix_len_ref[request] + page_len - 1, page_len)


def pack_kernel(
    nodes, per_node, most_pages, page_len, messages,
    request_ref, len_ref, holder_ref, slot_ref, node_ref, pool_ref, new_ref, decode_ref,
    *rest,
):
    page_out = rest[: len(messages)]
    decode_out = rest[len(messages) : len(messages) + nodes - 1]
    page_sem, decode_sem = rest[len(messages) + nodes - 1 :]
    me = node_ref[0]

    def page_copy(index, offset, slot):
        k, first, _ = messages[index]
        return pltpu.make_async_copy(
            pool_ref.at[:, slot], page_out[index].at[offset], page_sem.at[k - 1, first + offset]
        )

    counts = []
    for k in range(1, nodes):
        there = lax.rem(me + k, nodes)
        arrival = jnp.int32(0)
        for member in range(per_node):
            request = request_ref[there * per_node + member]
            page_total = pages_of(len_ref, request, page_len)

            def one_page(j, arrival, k=k, request=request):
                here = holder_ref[request, j] == me

                @pl.when(here)
                def _():
                    slot = slot_ref[request, j]
                    for index, (shift, first, last) in enumerate(messages):
                        if shift == k:

                            @pl.when((arrival >= first) & (arrival < last))
                            def _():
                                page_copy(index, arrival - first, slot).start()

                return arrival + here.astype(jnp.int32)

            arrival = lax.fori_loop(0, page_total, one_page, arrival)
        counts.append(arrival)

    def decode_copies(act):
        for k in range(1, nodes):
            there = lax.rem(me + k, nodes)
            for member in range(per_node):
                target = decode_ref[request_ref[me * per_node + member]]

                @pl.when(lax.div(target, per_node) == there)
                def _():
                    act(
                        pltpu.make_async_copy(
                            new_ref.at[:, member], decode_out[k - 1], decode_sem.at[k - 1]
                        )
                    )

    decode_copies(lambda copy: copy.start())
    for index, (k, first, last) in enumerate(messages):
        for offset in range(last - first):

            @pl.when(first + offset < counts[k - 1])
            def _():
                page_copy(index, offset, 0).wait()

    decode_copies(lambda copy: copy.wait())


def hand_kernel(
    nodes, per_node, request_ref, decode_ref, node_ref, new_ref, *rest
):
    arrived = rest[: nodes - 1]
    out_ref, sem = rest[nodes - 1 :]
    me = node_ref[0]

    def copies(act):
        def one_slot(p, carry):
            target = decode_ref[request_ref[p]]
            wanted = target - me * per_node

            @pl.when((wanted >= 0) & (wanted < per_node))
            def _():
                shift = lax.rem(me - lax.div(p, per_node) + nodes, nodes)
                for k in range(nodes):

                    @pl.when(shift == k)
                    def _():
                        source = new_ref.at[:, lax.rem(p, per_node)] if k == 0 else arrived[k - 1]
                        act(pltpu.make_async_copy(source, out_ref.at[:, wanted], sem.at[wanted]))

            return carry

        lax.fori_loop(0, nodes * per_node, one_slot, 0)

    copies(lambda copy: copy.start())
    copies(lambda copy: copy.wait())


def attend_kernel(
    nodes, per_node, most_pages, page_len, messages, opening, closing,
    request_ref, len_ref, holder_ref, slot_ref, node_ref, query_ref, *rest,
):
    if opening:
        new_ref, pool_ref = rest[:2]
        rest = rest[2:]
    else:
        old_acc, old_top, old_total = rest[:3]
        received = rest[3 : 3 + len(messages)]
        rest = rest[3 + len(messages) :]
    if closing:
        out_ref, acc_ref, top_ref, total_ref = rest[:4]
        rest = rest[4:]
    else:
        acc_ref, top_ref, total_ref = rest[:3]
        rest = rest[3:]
    page_ref, turned_ref, arrival_ref, page_sem = rest
    me = node_ref[0]
    width = page_ref.shape[-1]
    groups = width // HD
    per_group = query_ref.shape[2] // width
    heads = groups * per_group
    suffix = query_ref.shape[1]
    block_keys = BLOCK_PAGES * page_len
    rate = HD ** (-0.5) * math.log2(math.e)

    for holder in range(nodes):
        arrival_ref[holder] = 0
    page_counts, key_counts = [], []
    for member in range(per_node):
        request = request_ref[me * per_node + member]
        page_total = pages_of(len_ref, request, page_len)

        def one_page(j, carry, request=request, member=member, page_total=page_total):
            count, keys = carry
            holder = holder_ref[request, j]
            arrival = arrival_ref[holder]
            arrival_ref[holder] = arrival + 1
            shift = lax.rem(me - holder + nodes, nodes)
            sem = page_sem.at[member, count]
            place = page_ref.at[member, count]
            if opening:
                taken = shift == 0

                @pl.when(taken)
                def _():
                    pltpu.make_async_copy(pool_ref.at[:, slot_ref[request, j]], place, sem).start()

            else:
                taken = jnp.bool_(False)
                for index, (k, first, last) in enumerate(messages):
                    match = (shift == k) & (arrival >= first) & (arrival < last)
                    taken = taken | match

                    @pl.when(match)
                    def _():
                        pltpu.make_async_copy(received[index].at[arrival - first], place, sem).start()

            filled = jnp.minimum(len_ref[request] - j * page_len, page_len)
            return (
                count + taken.astype(jnp.int32),
                keys + jnp.where(taken, filled, 0),
            )

        count, keys = lax.fori_loop(0, page_total, one_page, (jnp.int32(0), jnp.int32(0)))
        page_counts.append(count)
        key_counts.append(keys)

    if opening:
        row = lax.broadcasted_iota(jnp.int32, (suffix, suffix), 0)
        column = lax.broadcasted_iota(jnp.int32, (suffix, suffix), 1)
        for member in range(per_node):
            for group in range(groups):
                lanes = slice(group * HD, (group + 1) * HD)
                keys_new = new_ref[0, member, :, lanes]
                values_new = new_ref[1, member, :, lanes].T

                def one_head(h, carry, member=member, group=group, keys_new=keys_new, values_new=values_new):
                    head = group * per_group + h
                    place = member * heads + head
                    query = query_ref[member, :, pl.ds(pl.multiple_of(head * HD, HD), HD)]
                    scores = lax.dot_general(
                        keys_new, query, (((1,), (1,)), ((), ())), preferred_element_type=jnp.float32
                    )
                    scores = jnp.where(row <= column, scores, MASKED)
                    top = jnp.max(scores, axis=0, keepdims=True)
                    weights = jnp.exp2((scores - top) * rate)
                    top_ref[place] = top
                    total_ref[place] = jnp.sum(weights, axis=0, keepdims=True)
                    acc_ref[place] = jnp.dot(
                        values_new, weights.astype(jnp.bfloat16), preferred_element_type=jnp.float32
                    )
                    return carry

                lax.fori_loop(0, per_group, one_head, 0, unroll=2)
    else:
        acc_ref[...] = old_acc[...]
        top_ref[...] = old_top[...]
        total_ref[...] = old_total[...]

    most_blocks = page_ref.shape[1] // BLOCK_PAGES
    for member in range(per_node):
        count, keys = page_counts[member], key_counts[member]

        def wait_page(i, carry, member=member):
            pltpu.make_async_copy(page_ref.at[member, i], page_ref.at[member, i], page_sem.at[member, i]).wait()
            return carry

        lax.fori_loop(0, count, wait_page, 0)
        blocks = lax.div(count + BLOCK_PAGES - 1, BLOCK_PAGES)

        def one_block(b, carry, member=member, count=count, keys=keys):
            pages = pl.ds(b * BLOCK_PAGES, BLOCK_PAGES)
            key_row = lax.broadcasted_iota(jnp.int32, (block_keys, 1), 0) + b * block_keys
            for group in range(groups):
                lanes = slice(group * HD, (group + 1) * HD)
                block_values = page_ref[member, pages, 1, :, lanes].reshape(block_keys, HD)
                block_values = jnp.where(key_row < keys, block_values, jnp.zeros_like(block_values))
                turned_ref[...] = block_values.T

                def one_head(h, carry, group=group, lanes=lanes):
                    head = group * per_group + h
                    place = member * heads + head
                    query = query_ref[member, :, pl.ds(pl.multiple_of(head * HD, HD), HD)]
                    block_key = page_ref[member, pages, 0, :, lanes].reshape(block_keys, HD)
                    scores = lax.dot_general(
                        block_key, query, (((1,), (1,)), ((), ())), preferred_element_type=jnp.float32
                    )
                    scores = jnp.where(key_row < keys, scores, MASKED)
                    before = top_ref[place]
                    top = jnp.maximum(before, jnp.max(scores, axis=0, keepdims=True))
                    weights = jnp.exp2((scores - top) * rate)
                    fade = jnp.exp2((before - top) * rate)
                    top_ref[place] = top
                    total_ref[place] = total_ref[place] * fade + jnp.sum(weights, axis=0, keepdims=True)
                    acc_ref[place] = acc_ref[place] * fade + jnp.dot(
                        turned_ref[...], weights.astype(jnp.bfloat16), preferred_element_type=jnp.float32
                    )
                    return carry

                lax.fori_loop(0, per_group, one_head, 0, unroll=2)
            return carry

        lax.fori_loop(0, blocks, one_block, 0)

    if closing:
        for member in range(per_node):

            def one_out(head, carry, member=member):
                place = member * heads + head
                result = acc_ref[place] / total_ref[place]
                out_ref[member, :, pl.ds(pl.multiple_of(head * HD, HD), HD)] = result.T.astype(out_ref.dtype)
                return carry

            lax.fori_loop(0, heads, one_out, 0, unroll=2)


def body(queries, new_kv, page_pool, slot_request, prefix_len, page_holder, page_slot, decode_slot):
    nodes = lax.axis_size("node")
    me = lax.axis_index("node").astype(jnp.int32).reshape(1)
    per_node, suffix, query_width = queries.shape
    page_len, width = page_pool.shape[2:]
    most_pages = page_holder.shape[1]
    capacity = page_pool.shape[1] // nodes
    heads = query_width // HD
    stages = message_plan(nodes, capacity)
    messages = [message for stage in stages for message in stage]
    tables = (slot_request, prefix_len, page_holder, page_slot, me)
    page_shape = (2, page_len, width)
    packed = pl.pallas_call(
        functools.partial(pack_kernel, nodes, per_node, most_pages, page_len, messages),
        grid_spec=pltpu.PrefetchScalarGridSpec(
            num_scalar_prefetch=5,
            grid=(),
            in_specs=[ANY, ANY, pl.BlockSpec(memory_space=pltpu.SMEM)],
            out_specs=[ANY] * (len(messages) + nodes - 1),
            scratch_shapes=[
                pltpu.SemaphoreType.DMA((max(nodes - 1, 1), capacity)),
                pltpu.SemaphoreType.DMA((max(nodes - 1, 1),)),
            ],
        ),
        out_shape=[jax.ShapeDtypeStruct((last - first,) + page_shape, page_pool.dtype) for _, first, last in messages]
        + [jax.ShapeDtypeStruct((2, suffix, width), new_kv.dtype)] * (nodes - 1),
        name="pack",
    )(*tables, page_pool, new_kv, decode_slot)

    def shifted(array, k):
        return lax.ppermute(array, "node", [(i, (i + k) % nodes) for i in range(nodes)])

    arrived = {message: shifted(packed[i], message[0]) for i, message in enumerate(messages)}
    handed = [shifted(packed[len(messages) + k - 1], k) for k in range(1, nodes)]

    state_shape = [
        jax.ShapeDtypeStruct((per_node * heads, HD, suffix), jnp.float32),
        jax.ShapeDtypeStruct((per_node * heads, 1, suffix), jnp.float32),
        jax.ShapeDtypeStruct((per_node * heads, 1, suffix), jnp.float32),
    ]

    def attend(stage, inputs, opening, closing):
        slots = capacity if opening else sum(last - first for _, first, last in stage)
        slots = -(-min(slots, most_pages) // BLOCK_PAGES) * BLOCK_PAGES
        in_specs = [VMEM] + ([VMEM, ANY] if opening else [VMEM] * 3 + [ANY] * len(stage))
        out_specs = [VMEM] * (4 if closing else 3)
        result_shape = ([jax.ShapeDtypeStruct(queries.shape, queries.dtype)] if closing else []) + state_shape
        scratch = [
            pltpu.VMEM((per_node, slots) + page_shape, page_pool.dtype),
            pltpu.VMEM((HD, BLOCK_PAGES * page_len), page_pool.dtype),
            pltpu.SMEM((nodes,), jnp.int32),
            pltpu.SemaphoreType.DMA((per_node, slots)),
        ]
        if closing:
            out_specs = [VMEM]
            result_shape = result_shape[:1]
            scratch = [pltpu.VMEM(s.shape, s.dtype) for s in state_shape] + scratch
        work = (slots + (per_node * 2 if opening else 0)) * page_len * heads * suffix
        return pl.pallas_call(
            functools.partial(
                attend_kernel, nodes, per_node, most_pages, page_len, stage, opening, closing
            ),
            grid_spec=pltpu.PrefetchScalarGridSpec(
                num_scalar_prefetch=5, grid=(), in_specs=in_specs, out_specs=out_specs, scratch_shapes=scratch
            ),
            out_shape=result_shape,
            compiler_params=pltpu.CompilerParams(vmem_limit_bytes=40 * 1024 * 1024),
            cost_estimate=pl.CostEstimate(
                flops=work * 4 * HD * 2, bytes_accessed=12 * 1024 * 1024, transcendentals=work
            ),
            name="attend",
        )(*tables, queries, *inputs)

    state = attend([], [new_kv, page_pool], True, not stages)
    for index, stage in enumerate(stages):
        state = attend(stage, list(state) + [arrived[m] for m in stage], False, index == len(stages) - 1)
    attended = state[0]
    decode_kv = pl.pallas_call(
        functools.partial(hand_kernel, nodes, per_node),
        grid_spec=pltpu.PrefetchScalarGridSpec(
            num_scalar_prefetch=3,
            grid=(),
            in_specs=[ANY] * nodes,
            out_specs=ANY,
            scratch_shapes=[pltpu.SemaphoreType.DMA((per_node,))],
        ),
        out_shape=jax.ShapeDtypeStruct(new_kv.shape, new_kv.dtype),
        name="hand",
    )(slot_request, decode_slot, me, new_kv, *handed)
    return attended, decode_kv


def solution(mesh):
    placed = (
        P(("groups", "node"), None, "tp"),
        P(None, ("groups", "node"), None, "tp"),
        P(None, ("groups", "node"), None, "tp"),
        P("groups"),
        P("groups"),
        P("groups", None),
        P("groups", None),
        P("groups"),
    )
    return jax.shard_map(
        body,
        mesh=mesh,
        in_specs=placed,
        out_specs=(P(("groups", "node"), None, "tp"), P(None, ("groups", "node"), None, "tp")),
        check_vma=False,
    )
```

```python
import functools
import math

import jax
import jax.numpy as jnp
from jax import lax
from jax.experimental import pallas as pl
from jax.experimental.pallas import tpu as pltpu
from jax.sharding import PartitionSpec as P

HD = 128
BLOCK_PAGES = 4
UNROLL = 8
MASKED = -1e30
ANY = pl.BlockSpec(memory_space=pl.ANY)
VMEM = pl.BlockSpec(memory_space=pltpu.VMEM)


def message_plan(nodes, capacity):
    half = nodes // 2
    others = [k for k in range(1, nodes) if k != half]
    cut = (capacity + 1) // 2
    stages = [[(half, 0, capacity)]] if nodes > 1 else []
    if others:
        stages.append([(k, 0, cut) for k in others])
        if cut < capacity:
            stages.append([(k, cut, capacity) for k in others])
    return stages


def pages_of(prefix_len_ref, request, page_len):
    return lax.div(prefix_len_ref[request] + page_len - 1, page_len)


def pack_kernel(
    nodes, per_node, most_pages, page_len, messages,
    request_ref, len_ref, holder_ref, slot_ref, node_ref, pool_ref, new_ref, decode_ref,
    *rest,
):
    page_out = rest[: len(messages)]
    decode_out = rest[len(messages) : len(messages) + nodes - 1]
    page_sem, decode_sem = rest[len(messages) + nodes - 1 :]
    me = node_ref[0]

    def page_copy(index, offset, slot):
        k, first, _ = messages[index]
        return pltpu.make_async_copy(
            pool_ref.at[:, slot], page_out[index].at[offset], page_sem.at[k - 1, first + offset]
        )

    counts = []
    for k in range(1, nodes):
        there = lax.rem(me + k, nodes)
        arrival = jnp.int32(0)
        for member in range(per_node):
            request = request_ref[there * per_node + member]
            page_total = pages_of(len_ref, request, page_len)

            def one_page(j, arrival, k=k, request=request):
                here = holder_ref[request, j] == me

                @pl.when(here)
                def _():
                    slot = slot_ref[request, j]
                    for index, (shift, first, last) in enumerate(messages):
                        if shift == k:

                            @pl.when((arrival >= first) & (arrival < last))
                            def _():
                                page_copy(index, arrival - first, slot).start()

                return arrival + here.astype(jnp.int32)

            arrival = lax.fori_loop(0, page_total, one_page, arrival)
        counts.append(arrival)

    def decode_copies(act):
        for k in range(1, nodes):
            there = lax.rem(me + k, nodes)
            for member in range(per_node):
                target = decode_ref[request_ref[me * per_node + member]]

                @pl.when(lax.div(target, per_node) == there)
                def _():
                    act(
                        pltpu.make_async_copy(
                            new_ref.at[:, member], decode_out[k - 1], decode_sem.at[k - 1]
                        )
                    )

    decode_copies(lambda copy: copy.start())
    for index, (k, first, last) in enumerate(messages):
        for offset in range(last - first):

            @pl.when(first + offset < counts[k - 1])
            def _():
                page_copy(index, offset, 0).wait()

    decode_copies(lambda copy: copy.wait())


def hand_kernel(
    nodes, per_node, request_ref, decode_ref, node_ref, new_ref, *rest
):
    arrived = rest[: nodes - 1]
    out_ref, sem = rest[nodes - 1 :]
    me = node_ref[0]

    def copies(act):
        def one_slot(p, carry):
            target = decode_ref[request_ref[p]]
            wanted = target - me * per_node

            @pl.when((wanted >= 0) & (wanted < per_node))
            def _():
                shift = lax.rem(me - lax.div(p, per_node) + nodes, nodes)
                for k in range(nodes):

                    @pl.when(shift == k)
                    def _():
                        source = new_ref.at[:, lax.rem(p, per_node)] if k == 0 else arrived[k - 1]
                        act(pltpu.make_async_copy(source, out_ref.at[:, wanted], sem.at[wanted]))

            return carry

        lax.fori_loop(0, nodes * per_node, one_slot, 0)

    copies(lambda copy: copy.start())
    copies(lambda copy: copy.wait())


def attend_kernel(
    nodes, per_node, most_pages, page_len, messages, opening, closing,
    request_ref, len_ref, holder_ref, slot_ref, node_ref, query_ref, *rest,
):
    if opening:
        new_ref, pool_ref = rest[:2]
        rest = rest[2:]
    else:
        old_acc, old_top, old_total = rest[:3]
        received = rest[3 : 3 + len(messages)]
        rest = rest[3 + len(messages) :]
    if closing:
        out_ref, acc_ref, top_ref, total_ref = rest[:4]
        rest = rest[4:]
    else:
        acc_ref, top_ref, total_ref = rest[:3]
        rest = rest[3:]
    page_ref, turned_ref, arrival_ref, page_sem = rest
    me = node_ref[0]
    width = page_ref.shape[-1]
    groups = width // HD
    per_group = query_ref.shape[2] // width
    heads = groups * per_group
    suffix = query_ref.shape[1]
    block_keys = BLOCK_PAGES * page_len
    rate = HD ** (-0.5) * math.log2(math.e)

    for holder in range(nodes):
        arrival_ref[holder] = 0
    page_counts, key_counts = [], []
    for member in range(per_node):
        request = request_ref[me * per_node + member]
        page_total = pages_of(len_ref, request, page_len)

        def one_page(j, carry, request=request, member=member, page_total=page_total):
            count, keys = carry
            holder = holder_ref[request, j]
            arrival = arrival_ref[holder]
            arrival_ref[holder] = arrival + 1
            shift = lax.rem(me - holder + nodes, nodes)
            sem = page_sem.at[member, count]
            place = page_ref.at[member, count]
            if opening:
                taken = shift == 0

                @pl.when(taken)
                def _():
                    pltpu.make_async_copy(pool_ref.at[:, slot_ref[request, j]], place, sem).start()

            else:
                taken = jnp.bool_(False)
                for index, (k, first, last) in enumerate(messages):
                    match = (shift == k) & (arrival >= first) & (arrival < last)
                    taken = taken | match

                    @pl.when(match)
                    def _():
                        pltpu.make_async_copy(received[index].at[arrival - first], place, sem).start()

            filled = jnp.minimum(len_ref[request] - j * page_len, page_len)
            return (
                count + taken.astype(jnp.int32),
                keys + jnp.where(taken, filled, 0),
            )

        count, keys = lax.fori_loop(0, page_total, one_page, (jnp.int32(0), jnp.int32(0)))
        page_counts.append(count)
        key_counts.append(keys)

    if opening:
        row = lax.broadcasted_iota(jnp.int32, (suffix, suffix), 0)
        column = lax.broadcasted_iota(jnp.int32, (suffix, suffix), 1)
        for member in range(per_node):
            for group in range(groups):
                lanes = slice(group * HD, (group + 1) * HD)
                keys_new = new_ref[0, member, :, lanes]
                values_new = new_ref[1, member, :, lanes].T

                def one_head(h, carry, member=member, group=group, keys_new=keys_new, values_new=values_new):
                    head = group * per_group + h
                    place = member * heads + head
                    query = query_ref[member, :, pl.ds(pl.multiple_of(head * HD, HD), HD)]
                    scores = lax.dot_general(
                        keys_new, query, (((1,), (1,)), ((), ())), preferred_element_type=jnp.float32
                    )
                    scores = jnp.where(row <= column, scores, MASKED)
                    top = jnp.max(scores, axis=0, keepdims=True)
                    weights = jnp.exp2((scores - top) * rate)
                    top_ref[place] = top
                    total_ref[place] = jnp.sum(weights, axis=0, keepdims=True)
                    acc_ref[place] = jnp.dot(
                        values_new, weights.astype(jnp.bfloat16), preferred_element_type=jnp.float32
                    )
                    return carry

                lax.fori_loop(0, per_group, one_head, 0, unroll=2)
    else:
        acc_ref[...] = old_acc[...]
        top_ref[...] = old_top[...]
        total_ref[...] = old_total[...]

    most_blocks = page_ref.shape[1] // BLOCK_PAGES
    for member in range(per_node):
        count, keys = page_counts[member], key_counts[member]

        def wait_page(i, carry, member=member):
            pltpu.make_async_copy(page_ref.at[member, i], page_ref.at[member, i], page_sem.at[member, i]).wait()
            return carry

        lax.fori_loop(0, count, wait_page, 0)
        blocks = lax.div(count + BLOCK_PAGES - 1, BLOCK_PAGES)

        def one_block(b, carry, member=member, keys=keys):
            pages = pl.ds(b * BLOCK_PAGES, BLOCK_PAGES)
            valid = keys - b * block_keys

            def heads_of_block(masked):
                for group in range(groups):
                    lanes = slice(group * HD, (group + 1) * HD)
                    block_values = page_ref[member, pages, 1, :, lanes].reshape(block_keys, HD)
                    if masked:
                        row = lax.broadcasted_iota(jnp.int32, (block_keys, HD), 0)
                        block_values = jnp.where(row < valid, block_values, jnp.zeros_like(block_values))
                    turned_ref[...] = block_values.T

                    def one_head(h, carry, group=group, lanes=lanes):
                        head = group * per_group + h
                        place = member * heads + head
                        query = query_ref[member, :, pl.ds(pl.multiple_of(head * HD, HD), HD)]
                        block_key = page_ref[member, pages, 0, :, lanes].reshape(block_keys, HD)
                        scores = lax.dot_general(
                            block_key, query, (((1,), (1,)), ((), ())), preferred_element_type=jnp.float32
                        )
                        if masked:
                            row = lax.broadcasted_iota(jnp.int32, scores.shape, 0)
                            scores = jnp.where(row < valid, scores, MASKED)
                        before = top_ref[place]
                        top = jnp.maximum(before, jnp.max(scores, axis=0, keepdims=True))
                        weights = jnp.exp2((scores - top) * rate)
                        fade = jnp.exp2((before - top) * rate)
                        top_ref[place] = top
                        total_ref[place] = total_ref[place] * fade + jnp.sum(weights, axis=0, keepdims=True)
                        acc_ref[place] = acc_ref[place] * fade + jnp.dot(
                            turned_ref[...], weights.astype(jnp.bfloat16), preferred_element_type=jnp.float32
                        )
                        return carry

                    lax.fori_loop(0, per_group, one_head, 0, unroll=UNROLL)

            @pl.when(valid >= block_keys)
            def _():
                heads_of_block(False)

            @pl.when(valid < block_keys)
            def _():
                heads_of_block(True)

            return carry

        lax.fori_loop(0, blocks, one_block, 0)

    if closing:
        for member in range(per_node):

            def one_out(head, carry, member=member):
                place = member * heads + head
                result = acc_ref[place] / total_ref[place]
                out_ref[member, :, pl.ds(pl.multiple_of(head * HD, HD), HD)] = result.T.astype(out_ref.dtype)
                return carry

            lax.fori_loop(0, heads, one_out, 0, unroll=2)


def attend(nodes, capacity, page_pool_dtype, page_shape, most_pages, tables, queries, stage, inputs, opening, closing):
    per_node, suffix, query_width = queries.shape
    page_len = page_shape[1]
    heads = query_width // HD
    state_shape = [
        jax.ShapeDtypeStruct((per_node * heads, HD, suffix), jnp.float32),
        jax.ShapeDtypeStruct((per_node * heads, 1, suffix), jnp.float32),
        jax.ShapeDtypeStruct((per_node * heads, 1, suffix), jnp.float32),
    ]

    slots = capacity if opening else sum(last - first for _, first, last in stage)
    slots = -(-min(slots, most_pages) // BLOCK_PAGES) * BLOCK_PAGES
    in_specs = [VMEM] + ([VMEM, ANY] if opening else [VMEM] * 3 + [ANY] * len(stage))
    out_specs = [VMEM] * (4 if closing else 3)
    result_shape = ([jax.ShapeDtypeStruct(queries.shape, queries.dtype)] if closing else []) + state_shape
    scratch = [
        pltpu.VMEM((per_node, slots) + page_shape, page_pool_dtype),
        pltpu.VMEM((HD, BLOCK_PAGES * page_len), page_pool_dtype),
        pltpu.SMEM((nodes,), jnp.int32),
        pltpu.SemaphoreType.DMA((per_node, slots)),
    ]
    if closing:
        out_specs = [VMEM]
        result_shape = result_shape[:1]
        scratch = [pltpu.VMEM(s.shape, s.dtype) for s in state_shape] + scratch
    work = (slots + (per_node * 2 if opening else 0)) * page_len * heads * suffix
    return pl.pallas_call(
        functools.partial(
            attend_kernel, nodes, per_node, most_pages, page_len, stage, opening, closing
        ),
        grid_spec=pltpu.PrefetchScalarGridSpec(
            num_scalar_prefetch=5, grid=(), in_specs=in_specs, out_specs=out_specs, scratch_shapes=scratch
        ),
        out_shape=result_shape,
        compiler_params=pltpu.CompilerParams(vmem_limit_bytes=40 * 1024 * 1024),
        cost_estimate=pl.CostEstimate(
            flops=work * 4 * HD * 2, bytes_accessed=12 * 1024 * 1024, transcendentals=work
        ),
        name="attend",
    )(*tables, queries, *inputs)


def body(queries, new_kv, page_pool, slot_request, prefix_len, page_holder, page_slot, decode_slot):
    nodes = lax.axis_size("node")
    me = lax.axis_index("node").astype(jnp.int32).reshape(1)
    per_node, suffix, query_width = queries.shape
    page_len, width = page_pool.shape[2:]
    most_pages = page_holder.shape[1]
    capacity = page_pool.shape[1] // nodes
    stages = message_plan(nodes, capacity)
    messages = [message for stage in stages for message in stage]
    tables = (slot_request, prefix_len, page_holder, page_slot, me)
    page_shape = (2, page_len, width)
    packed = pl.pallas_call(
        functools.partial(pack_kernel, nodes, per_node, most_pages, page_len, messages),
        grid_spec=pltpu.PrefetchScalarGridSpec(
            num_scalar_prefetch=5,
            grid=(),
            in_specs=[ANY, ANY, pl.BlockSpec(memory_space=pltpu.SMEM)],
            out_specs=[VMEM] * (len(messages) + nodes - 1),
            scratch_shapes=[
                pltpu.SemaphoreType.DMA((max(nodes - 1, 1), capacity)),
                pltpu.SemaphoreType.DMA((max(nodes - 1, 1),)),
            ],
        ),
        out_shape=[jax.ShapeDtypeStruct((last - first,) + page_shape, page_pool.dtype) for _, first, last in messages]
        + [jax.ShapeDtypeStruct((2, suffix, width), new_kv.dtype)] * (nodes - 1),
        name="pack",
    )(*tables, page_pool, new_kv, decode_slot)

    def shifted(array, k):
        return lax.ppermute(array, "node", [(i, (i + k) % nodes) for i in range(nodes)])

    arrived = {message: shifted(packed[i], message[0]) for i, message in enumerate(messages)}
    outgoing = packed[len(messages) :]
    if stages:
        first = stages[0][0]
        arrived[first], outgoing = lax.optimization_barrier((arrived[first], outgoing))
    handed = [shifted(outgoing[k - 1], k) for k in range(1, nodes)]

    attending = functools.partial(
        attend, nodes, capacity, page_pool.dtype, page_shape, most_pages, tables, queries
    )
    state = attending([], [new_kv, page_pool], True, not stages)
    for index, stage in enumerate(stages):
        state = attending(stage, list(state) + [arrived[m] for m in stage], False, index == len(stages) - 1)
    attended = state[0]
    decode_kv = pl.pallas_call(
        functools.partial(hand_kernel, nodes, per_node),
        grid_spec=pltpu.PrefetchScalarGridSpec(
            num_scalar_prefetch=3,
            grid=(),
            in_specs=[ANY] * nodes,
            out_specs=VMEM,
            scratch_shapes=[pltpu.SemaphoreType.DMA((per_node,))],
        ),
        out_shape=jax.ShapeDtypeStruct(new_kv.shape, new_kv.dtype),
        name="hand",
    )(slot_request, decode_slot, me, new_kv, *handed)
    return attended, decode_kv


def solution(mesh):
    placed = (
        P(("groups", "node"), None, "tp"),
        P(None, ("groups", "node"), None, "tp"),
        P(None, ("groups", "node"), None, "tp"),
        P("groups"),
        P("groups"),
        P("groups", None),
        P("groups", None),
        P("groups"),
    )
    return jax.shard_map(
        body,
        mesh=mesh,
        in_specs=placed,
        out_specs=(P(("groups", "node"), None, "tp"), P(None, ("groups", "node"), None, "tp")),
        check_vma=False,
    )
```

```python
import functools
import math

import jax
import jax.numpy as jnp
from jax import lax
from jax.experimental import pallas as pl
from jax.experimental.pallas import tpu as pltpu
from jax.sharding import PartitionSpec as P

HD = 128
BLOCK_PAGES = 4
MASKED = -1e30
ANY = pl.BlockSpec(memory_space=pl.ANY)
VMEM = pl.BlockSpec(memory_space=pltpu.VMEM)


def message_plan(nodes, capacity):
    half = nodes // 2
    shifts = [half] * (nodes > 1) + [k for k in range(1, nodes) if k != half]
    cut = (capacity + 1) // 2
    stages = [[(k, 0, cut) for k in shifts]] if shifts else []
    if cut < capacity and shifts:
        stages.append([(k, cut, capacity) for k in shifts])
    return stages


def pages_of(prefix_len_ref, request, page_len):
    return lax.div(prefix_len_ref[request] + page_len - 1, page_len)


def pack_kernel(
    nodes, per_node, most_pages, page_len, messages,
    request_ref, len_ref, holder_ref, slot_ref, node_ref, pool_ref, new_ref, decode_ref,
    *rest,
):
    page_out = rest[: len(messages)]
    decode_out = rest[len(messages) : len(messages) + nodes - 1]
    page_sem, decode_sem = rest[len(messages) + nodes - 1 :]
    me = node_ref[0]

    def page_copy(index, offset, slot):
        k, first, _ = messages[index]
        return pltpu.make_async_copy(
            pool_ref.at[:, slot], page_out[index].at[offset], page_sem.at[k - 1, first + offset]
        )

    counts = []
    for k in range(1, nodes):
        there = lax.rem(me + k, nodes)
        arrival = jnp.int32(0)
        for member in range(per_node):
            request = request_ref[there * per_node + member]
            page_total = pages_of(len_ref, request, page_len)

            def one_page(j, arrival, k=k, request=request):
                here = holder_ref[request, j] == me

                @pl.when(here)
                def _():
                    slot = slot_ref[request, j]
                    for index, (shift, first, last) in enumerate(messages):
                        if shift == k:

                            @pl.when((arrival >= first) & (arrival < last))
                            def _():
                                page_copy(index, arrival - first, slot).start()

                return arrival + here.astype(jnp.int32)

            arrival = lax.fori_loop(0, page_total, one_page, arrival)
        counts.append(arrival)

    def decode_copies(act):
        for k in range(1, nodes):
            there = lax.rem(me + k, nodes)
            for member in range(per_node):
                target = decode_ref[request_ref[me * per_node + member]]

                @pl.when(lax.div(target, per_node) == there)
                def _():
                    act(
                        pltpu.make_async_copy(
                            new_ref.at[:, member], decode_out[k - 1], decode_sem.at[k - 1]
                        )
                    )

    decode_copies(lambda copy: copy.start())

    for index, (k, first, last) in enumerate(messages):
        for offset in range(last - first):

            @pl.when(first + offset < counts[k - 1])
            def _():
                page_copy(index, offset, 0).wait()

    decode_copies(lambda copy: copy.wait())


def hand_kernel(
    nodes, per_node, request_ref, decode_ref, node_ref, new_ref, *rest
):
    arrived = rest[: nodes - 1]
    out_ref, sem = rest[nodes - 1 :]
    me = node_ref[0]

    def copies(act):
        def one_slot(p, carry):
            target = decode_ref[request_ref[p]]
            wanted = target - me * per_node

            @pl.when((wanted >= 0) & (wanted < per_node))
            def _():
                shift = lax.rem(me - lax.div(p, per_node) + nodes, nodes)
                for k in range(nodes):

                    @pl.when(shift == k)
                    def _():
                        source = new_ref.at[:, lax.rem(p, per_node)] if k == 0 else arrived[k - 1]
                        act(pltpu.make_async_copy(source, out_ref.at[:, wanted], sem.at[wanted]))

            return carry

        lax.fori_loop(0, nodes * per_node, one_slot, 0)

    copies(lambda copy: copy.start())
    copies(lambda copy: copy.wait())


def head_pipeline(count, scores_of, place_of, top_ref, total_ref, acc_ref, score_ref, weight_ref, turned, rate, fresh, visible):
    def soften(h):
        place = place_of(h)
        scores = visible(score_ref[h % 2])
        top = jnp.max(scores, axis=0, keepdims=True)
        if not fresh:
            before = top_ref[place]
            top = jnp.maximum(before, top)
            fade = jnp.exp2((before - top) * rate)
            fade_of[h] = fade
        weights = jnp.exp2((scores - top) * rate)
        total = jnp.sum(weights, axis=0, keepdims=True)
        top_ref[place] = top
        total_ref[place] = total if fresh else total_ref[place] * fade + total
        weight_ref[h % 2] = weights.astype(weight_ref.dtype)

    def gather(h):
        place = place_of(h)
        product = jnp.dot(turned, weight_ref[h % 2], preferred_element_type=jnp.float32)
        acc_ref[place] = product if fresh else acc_ref[place] * fade_of[h] + product

    fade_of = {}
    for step in range(count + 2):
        if step < count:
            score_ref[step % 2] = scores_of(step)
        if 0 <= step - 2 < count:
            gather(step - 2)
        if 0 <= step - 1 < count:
            soften(step - 1)


def attend_kernel(
    nodes, per_node, most_pages, page_len, messages, opening, closing,
    request_ref, len_ref, holder_ref, slot_ref, node_ref, query_ref, *rest,
):
    if opening:
        new_ref, pool_ref = rest[:2]
        rest = rest[2:]
    else:
        old_acc, old_top, old_total = rest[:3]
        received = rest[3 : 3 + len(messages)]
        rest = rest[3 + len(messages) :]
    if closing:
        out_ref, acc_ref, top_ref, total_ref = rest[:4]
        rest = rest[4:]
    else:
        acc_ref, top_ref, total_ref = rest[:3]
        rest = rest[3:]
    page_ref, score_ref, weight_ref, arrival_ref, count_ref, page_sem = rest
    me = node_ref[0]
    width = page_ref.shape[-1]
    groups = width // HD
    per_group = query_ref.shape[2] // width
    heads = groups * per_group
    suffix = query_ref.shape[1]
    block_keys = BLOCK_PAGES * page_len
    rate = HD ** (-0.5) * math.log2(math.e)

    for holder in range(nodes):
        arrival_ref[holder] = 0
    for member in range(per_node):
        request = request_ref[me * per_node + member]

        def one_page(j, carry, request=request, member=member):
            count, keys = carry
            holder = holder_ref[request, j]
            arrival = arrival_ref[holder]
            arrival_ref[holder] = arrival + 1
            shift = lax.rem(me - holder + nodes, nodes)
            sem = page_sem.at[member, count]
            place = page_ref.at[member, count]
            if opening:
                taken = shift == 0

                @pl.when(taken)
                def _():
                    pltpu.make_async_copy(pool_ref.at[:, slot_ref[request, j]], place, sem).start()

            else:
                taken = jnp.bool_(False)
                for index, (k, first, last) in enumerate(messages):
                    match = (shift == k) & (arrival >= first) & (arrival < last)
                    taken = taken | match

                    @pl.when(match)
                    def _():
                        pltpu.make_async_copy(received[index].at[arrival - first], place, sem).start()

            filled = jnp.minimum(len_ref[request] - j * page_len, page_len)
            return (
                count + taken.astype(jnp.int32),
                keys + jnp.where(taken, filled, 0),
            )

        count, keys = lax.fori_loop(
            0, pages_of(len_ref, request, page_len), one_page, (jnp.int32(0), jnp.int32(0))
        )
        count_ref[0, member] = count
        count_ref[1, member] = keys

    def head_lanes(group, h):
        return pl.ds(pl.multiple_of((group * per_group + h) * HD, HD), HD)

    def over_groups(act):
        def one_group(i, carry):
            member, group = lax.div(i, groups), lax.rem(i, groups)
            act(member, group, pl.ds(pl.multiple_of(group * HD, HD), HD))
            return carry

        lax.fori_loop(0, per_node * groups, one_group, 0)

    if opening:
        row = lax.broadcasted_iota(jnp.int32, (suffix, suffix), 0)
        column = lax.broadcasted_iota(jnp.int32, (suffix, suffix), 1)

        def new_keys(member, group, lanes):
            keys_new = new_ref[0, member, :, lanes]
            values_new = new_ref[1, member, :, lanes].T

            def scores_of(h):
                query = query_ref[member, :, head_lanes(group, h)]
                return lax.dot_general(
                    keys_new, query, (((1,), (1,)), ((), ())), preferred_element_type=jnp.float32
                )

            head_pipeline(
                per_group, scores_of, lambda h: member * heads + group * per_group + h,
                top_ref, total_ref, acc_ref, score_ref.at[:, :suffix], weight_ref.at[:, :suffix], values_new, rate, True,
                lambda scores: jnp.where(row <= column, scores, MASKED),
            )

        over_groups(new_keys)
    else:
        acc_ref[...] = old_acc[...]
        top_ref[...] = old_top[...]
        total_ref[...] = old_total[...]

    def wait_member(member, carry):
        def wait_page(i, carry):
            pltpu.make_async_copy(page_ref.at[member, i], page_ref.at[member, i], page_sem.at[member, i]).wait()
            return carry

        return lax.fori_loop(0, count_ref[0, member], wait_page, carry)

    lax.fori_loop(0, per_node, wait_member, 0)

    def old_keys(member, group, lanes):
        def one_block(b, carry):
            pages = pl.ds(b * BLOCK_PAGES, BLOCK_PAGES)
            valid = count_ref[1, member] - b * block_keys

            block_key = page_ref[member, pages, 0, :, lanes].reshape(block_keys, HD)
            block_values = page_ref[member, pages, 1, :, lanes].reshape(block_keys, HD)
            row = lax.broadcasted_iota(jnp.int32, (block_keys, HD), 0)
            block_values = jnp.where(row < valid, block_values, jnp.zeros_like(block_values))

            def scores_of(h):
                query = query_ref[member, :, head_lanes(group, h)]
                return lax.dot_general(
                    block_key, query, (((1,), (1,)), ((), ())), preferred_element_type=jnp.float32
                )

            def visible(scores):
                row = lax.broadcasted_iota(jnp.int32, scores.shape, 0)
                return jnp.where(row < valid, scores, MASKED)

            head_pipeline(
                per_group, scores_of, lambda h: member * heads + group * per_group + h,
                top_ref, total_ref, acc_ref, score_ref, weight_ref, block_values.T, rate, False, visible,
            )
            return carry

        lax.fori_loop(0, lax.div(count_ref[0, member] + BLOCK_PAGES - 1, BLOCK_PAGES), one_block, 0)

    over_groups(old_keys)

    if closing:
        for member in range(per_node):

            def one_out(head, carry, member=member):
                place = member * heads + head
                result = acc_ref[place] / total_ref[place]
                out_ref[member, :, pl.ds(pl.multiple_of(head * HD, HD), HD)] = result.T.astype(out_ref.dtype)
                return carry

            lax.fori_loop(0, heads, one_out, 0, unroll=2)


def attend(nodes, capacity, page_pool_dtype, page_shape, most_pages, tables, queries, stage, inputs, opening, closing):
    per_node, suffix, query_width = queries.shape
    page_len = page_shape[1]
    heads = query_width // HD
    state_shape = [
        jax.ShapeDtypeStruct((per_node * heads, HD, suffix), jnp.float32),
        jax.ShapeDtypeStruct((per_node * heads, 1, suffix), jnp.float32),
        jax.ShapeDtypeStruct((per_node * heads, 1, suffix), jnp.float32),
    ]

    slots = capacity if opening else sum(last - first for _, first, last in stage)
    slots = -(-min(slots, most_pages) // BLOCK_PAGES) * BLOCK_PAGES
    in_specs = [VMEM] + ([VMEM, ANY] if opening else [VMEM] * 3 + [ANY] * len(stage))
    out_specs = [VMEM] * (4 if closing else 3)
    result_shape = ([jax.ShapeDtypeStruct(queries.shape, queries.dtype)] if closing else []) + state_shape
    scratch = [
        pltpu.VMEM((per_node, slots) + page_shape, page_pool_dtype),
        pltpu.VMEM((2, BLOCK_PAGES * page_len, suffix), jnp.float32),
        pltpu.VMEM((2, BLOCK_PAGES * page_len, suffix), page_pool_dtype),
        pltpu.SMEM((nodes,), jnp.int32),
        pltpu.SMEM((2, per_node), jnp.int32),
        pltpu.SemaphoreType.DMA((per_node, slots)),
    ]
    if closing:
        out_specs = [VMEM]
        result_shape = result_shape[:1]
        scratch = [pltpu.VMEM(s.shape, s.dtype) for s in state_shape] + scratch
    work = (slots + (per_node * 2 if opening else 0)) * page_len * heads * suffix
    return pl.pallas_call(
        functools.partial(
            attend_kernel, nodes, per_node, most_pages, page_len, stage, opening, closing
        ),
        grid_spec=pltpu.PrefetchScalarGridSpec(
            num_scalar_prefetch=5, grid=(), in_specs=in_specs, out_specs=out_specs, scratch_shapes=scratch
        ),
        out_shape=result_shape,
        compiler_params=pltpu.CompilerParams(vmem_limit_bytes=40 * 1024 * 1024),
        cost_estimate=pl.CostEstimate(
            flops=work * 4 * HD * 2, bytes_accessed=12 * 1024 * 1024, transcendentals=work
        ),
        name="attend",
    )(*tables, queries, *inputs)


def body(queries, new_kv, page_pool, slot_request, prefix_len, page_holder, page_slot, decode_slot):
    nodes = lax.axis_size("node")
    me = lax.axis_index("node").astype(jnp.int32).reshape(1)
    per_node, suffix, query_width = queries.shape
    page_len, width = page_pool.shape[2:]
    most_pages = page_holder.shape[1]
    capacity = page_pool.shape[1] // nodes
    stages = message_plan(nodes, capacity)
    messages = [message for stage in stages for message in stage]
    tables = (slot_request, prefix_len, page_holder, page_slot, me)
    page_shape = (2, page_len, width)
    packed = pl.pallas_call(
        functools.partial(pack_kernel, nodes, per_node, most_pages, page_len, messages),
        grid_spec=pltpu.PrefetchScalarGridSpec(
            num_scalar_prefetch=5,
            grid=(),
            in_specs=[ANY, ANY, pl.BlockSpec(memory_space=pltpu.SMEM)],
            out_specs=[VMEM] * (len(messages) + nodes - 1),
            scratch_shapes=[
                pltpu.SemaphoreType.DMA((max(nodes - 1, 1), capacity)),
                pltpu.SemaphoreType.DMA((max(nodes - 1, 1),)),
            ],
        ),
        out_shape=[jax.ShapeDtypeStruct((last - first,) + page_shape, page_pool.dtype) for _, first, last in messages]
        + [jax.ShapeDtypeStruct((2, suffix, width), new_kv.dtype)] * (nodes - 1),
        name="pack",
    )(*tables, page_pool, new_kv, decode_slot)

    waiting = dict(zip(messages, packed))
    handing = packed[len(messages) :]
    attending = functools.partial(
        attend, nodes, capacity, page_pool.dtype, page_shape, most_pages, tables, queries
    )

    def shifted(array, k):
        return lax.ppermute(array, "node", [(i, (i + k) % nodes) for i in range(nodes)])

    def send_after(earlier, array, k):
        if earlier is not None:
            arrived[earlier], array = lax.optimization_barrier((arrived[earlier], array))
        return shifted(array, k)

    arrived, latest, handed = {}, {}, {}
    for stage in stages:
        for message in stage:
            k = message[0]
            arrived[message] = send_after(latest.get(k), waiting[message], k)
            latest[k] = message
    for k in latest:
        handed[k] = send_after(latest[k], handing[k - 1], k)

    state = attending([], [new_kv, page_pool], True, not stages)
    for index, stage in enumerate(stages):
        inputs = list(state) + [arrived[message] for message in stage]
        state = attending(stage, inputs, False, index == len(stages) - 1)
    decode_kv = pl.pallas_call(
        functools.partial(hand_kernel, nodes, per_node),
        grid_spec=pltpu.PrefetchScalarGridSpec(
            num_scalar_prefetch=3,
            grid=(),
            in_specs=[ANY] * nodes,
            out_specs=VMEM,
            scratch_shapes=[pltpu.SemaphoreType.DMA((per_node,))],
        ),
        out_shape=jax.ShapeDtypeStruct(new_kv.shape, new_kv.dtype),
        name="hand",
    )(slot_request, decode_slot, me, new_kv, *[handed[k] for k in range(1, nodes)])
    return state[0], decode_kv


def solution(mesh):
    placed = (
        P(("groups", "node"), None, "tp"),
        P(None, ("groups", "node"), None, "tp"),
        P(None, ("groups", "node"), None, "tp"),
        P("groups"),
        P("groups"),
        P("groups", None),
        P("groups", None),
        P("groups"),
    )
    return jax.shard_map(
        body,
        mesh=mesh,
        in_specs=placed,
        out_specs=(P(("groups", "node"), None, "tp"), P(None, ("groups", "node"), None, "tp")),
        check_vma=False,
    )
```

```python
import functools
import math

import jax
import jax.numpy as jnp
from jax import lax
from jax.experimental import pallas as pl
from jax.experimental.pallas import tpu as pltpu
from jax.sharding import PartitionSpec as P

HD = 128
BLOCK_PAGES = 4
MASKED = -1e30
ANY = pl.BlockSpec(memory_space=pl.ANY)
VMEM = pl.BlockSpec(memory_space=pltpu.VMEM)


def message_plan(nodes, capacity):
    half = nodes // 2
    shifts = [half] * (nodes > 1) + [k for k in range(1, nodes) if k != half]
    cut = (capacity + 1) // 2
    stages = [[(k, 0, cut) for k in shifts]] if shifts else []
    if cut < capacity and shifts:
        stages.append([(k, cut, capacity) for k in shifts])
    return stages


def pages_of(prefix_len_ref, request, page_len):
    return lax.div(prefix_len_ref[request] + page_len - 1, page_len)


def pack_kernel(
    nodes, per_node, most_pages, page_len, messages,
    request_ref, len_ref, holder_ref, slot_ref, node_ref, pool_ref, new_ref, decode_ref,
    *rest,
):
    page_out = rest[: len(messages)]
    decode_out = rest[len(messages) : len(messages) + nodes - 1]
    source_ref, page_sem, decode_sem = rest[len(messages) + nodes - 1 :]
    me = node_ref[0]

    def page_copy(index, offset, slot):
        k, first, _ = messages[index]
        return pltpu.make_async_copy(
            pool_ref.at[:, slot], page_out[index].at[offset], page_sem.at[k - 1, first + offset]
        )

    counts = []
    for k in range(1, nodes):
        there = lax.rem(me + k, nodes)
        arrival = jnp.int32(0)
        for member in range(per_node):
            request = request_ref[there * per_node + member]
            page_total = pages_of(len_ref, request, page_len)

            def one_page(j, arrival, k=k, request=request):
                here = holder_ref[request, j] == me

                @pl.when(here)
                def _():
                    slot = slot_ref[request, j]
                    for index, (shift, first, last) in enumerate(messages):
                        if shift == k:

                            @pl.when((arrival >= first) & (arrival < last))
                            def _():
                                page_copy(index, arrival - first, slot).start()

                return arrival + here.astype(jnp.int32)

            arrival = lax.fori_loop(0, page_total, one_page, arrival)
        counts.append(arrival)

    def decode_copies(act):
        for k in range(1, nodes):
            there = lax.rem(me + k, nodes)
            for member in range(per_node):
                target = decode_ref[request_ref[me * per_node + member]]

                @pl.when(lax.div(target, per_node) == there)
                def _():
                    act(
                        pltpu.make_async_copy(
                            new_ref.at[:, member], decode_out[k - 1], decode_sem.at[k - 1]
                        )
                    )

    decode_copies(lambda copy: copy.start())

    def one_source(p, carry):
        wanted = decode_ref[request_ref[p]] - me * per_node

        @pl.when((wanted >= 0) & (wanted < per_node))
        def _():
            source_ref[2 * wanted] = lax.rem(me - lax.div(p, per_node) + nodes, nodes)
            source_ref[2 * wanted + 1] = lax.rem(p, per_node)

        return carry

    lax.fori_loop(0, nodes * per_node, one_source, 0)

    for index, (k, first, last) in enumerate(messages):
        for offset in range(last - first):

            @pl.when(first + offset < counts[k - 1])
            def _():
                page_copy(index, offset, 0).wait()

    decode_copies(lambda copy: copy.wait())


def head_pipeline(count, scores_of, place_of, top_ref, total_ref, acc_ref, score_ref, weight_ref, turned, rate, fresh, visible):
    def soften(h):
        place = place_of(h)
        scores = visible(score_ref[h % 2])
        top = jnp.max(scores, axis=0, keepdims=True)
        if not fresh:
            before = top_ref[place]
            top = jnp.maximum(before, top)
            fade = jnp.exp2((before - top) * rate)
            fade_of[h] = fade
        weights = jnp.exp2((scores - top) * rate)
        total = jnp.sum(weights, axis=0, keepdims=True)
        top_ref[place] = top
        total_ref[place] = total if fresh else total_ref[place] * fade + total
        weight_ref[h % 2] = weights.astype(weight_ref.dtype)

    def gather(h):
        place = place_of(h)
        product = jnp.dot(turned, weight_ref[h % 2], preferred_element_type=jnp.float32)
        acc_ref[place] = product if fresh else acc_ref[place] * fade_of[h] + product

    fade_of = {}
    for step in range(count + 2):
        if step < count:
            score_ref[step % 2] = scores_of(step)
        if 0 <= step - 2 < count:
            gather(step - 2)
        if 0 <= step - 1 < count:
            soften(step - 1)


def attend_kernel(
    nodes, per_node, most_pages, page_len, messages, opening, closing,
    request_ref, len_ref, holder_ref, slot_ref, node_ref, query_ref, *rest,
):
    if opening:
        new_ref, pool_ref = rest[:2]
        rest = rest[2:]
    else:
        old_acc, old_top, old_total = rest[:3]
        received = rest[3 : 3 + len(messages)]
        rest = rest[3 + len(messages) :]
    if closing:
        out_ref, acc_ref, top_ref, total_ref = rest[:4]
        rest = rest[4:]
    else:
        acc_ref, top_ref, total_ref = rest[:3]
        rest = rest[3:]
    page_ref, score_ref, weight_ref, arrival_ref, count_ref, page_sem = rest
    me = node_ref[0]
    width = page_ref.shape[-1]
    groups = width // HD
    per_group = query_ref.shape[2] // width
    heads = groups * per_group
    suffix = query_ref.shape[1]
    block_keys = BLOCK_PAGES * page_len
    rate = HD ** (-0.5) * math.log2(math.e)

    for holder in range(nodes):
        arrival_ref[holder] = 0
    for member in range(per_node):
        request = request_ref[me * per_node + member]

        def one_page(j, carry, request=request, member=member):
            count, keys = carry
            holder = holder_ref[request, j]
            arrival = arrival_ref[holder]
            arrival_ref[holder] = arrival + 1
            shift = lax.rem(me - holder + nodes, nodes)
            sem = page_sem.at[member, count]
            place = page_ref.at[member, count]
            if opening:
                taken = shift == 0

                @pl.when(taken)
                def _():
                    pltpu.make_async_copy(pool_ref.at[:, slot_ref[request, j]], place, sem).start()

            else:
                taken = jnp.bool_(False)
                for index, (k, first, last) in enumerate(messages):
                    match = (shift == k) & (arrival >= first) & (arrival < last)
                    taken = taken | match

                    @pl.when(match)
                    def _():
                        pltpu.make_async_copy(received[index].at[arrival - first], place, sem).start()

            filled = jnp.minimum(len_ref[request] - j * page_len, page_len)
            return (
                count + taken.astype(jnp.int32),
                keys + jnp.where(taken, filled, 0),
            )

        count, keys = lax.fori_loop(
            0, pages_of(len_ref, request, page_len), one_page, (jnp.int32(0), jnp.int32(0))
        )
        count_ref[0, member] = count
        count_ref[1, member] = keys

    def head_lanes(group, h):
        return pl.ds(pl.multiple_of((group * per_group + h) * HD, HD), HD)

    def over_groups(act):
        def one_group(i, carry):
            member, group = lax.div(i, groups), lax.rem(i, groups)
            act(member, group, pl.ds(pl.multiple_of(group * HD, HD), HD))
            return carry

        lax.fori_loop(0, per_node * groups, one_group, 0)

    if opening:
        row = lax.broadcasted_iota(jnp.int32, (suffix, suffix), 0)
        column = lax.broadcasted_iota(jnp.int32, (suffix, suffix), 1)

        def new_keys(member, group, lanes):
            keys_new = new_ref[0, member, :, lanes]
            values_new = new_ref[1, member, :, lanes].T

            def scores_of(h):
                query = query_ref[member, :, head_lanes(group, h)]
                return lax.dot_general(
                    keys_new, query, (((1,), (1,)), ((), ())), preferred_element_type=jnp.float32
                )

            head_pipeline(
                per_group, scores_of, lambda h: member * heads + group * per_group + h,
                top_ref, total_ref, acc_ref, score_ref.at[:, :suffix], weight_ref.at[:, :suffix], values_new, rate, True,
                lambda scores: jnp.where(row <= column, scores, MASKED),
            )

        over_groups(new_keys)
    else:
        acc_ref[...] = old_acc[...]
        top_ref[...] = old_top[...]
        total_ref[...] = old_total[...]

    def wait_member(member, carry):
        def wait_page(i, carry):
            pltpu.make_async_copy(page_ref.at[member, i], page_ref.at[member, i], page_sem.at[member, i]).wait()
            return carry

        return lax.fori_loop(0, count_ref[0, member], wait_page, carry)

    lax.fori_loop(0, per_node, wait_member, 0)

    def old_keys(member, group, lanes):
        def one_block(b, carry):
            pages = pl.ds(b * BLOCK_PAGES, BLOCK_PAGES)
            valid = count_ref[1, member] - b * block_keys

            block_key = page_ref[member, pages, 0, :, lanes].reshape(block_keys, HD)
            block_values = page_ref[member, pages, 1, :, lanes].reshape(block_keys, HD)
            row = lax.broadcasted_iota(jnp.int32, (block_keys, HD), 0)
            block_values = jnp.where(row < valid, block_values, jnp.zeros_like(block_values))

            def scores_of(h):
                query = query_ref[member, :, head_lanes(group, h)]
                return lax.dot_general(
                    block_key, query, (((1,), (1,)), ((), ())), preferred_element_type=jnp.float32
                )

            def visible(scores):
                row = lax.broadcasted_iota(jnp.int32, scores.shape, 0)
                return jnp.where(row < valid, scores, MASKED)

            head_pipeline(
                per_group, scores_of, lambda h: member * heads + group * per_group + h,
                top_ref, total_ref, acc_ref, score_ref, weight_ref, block_values.T, rate, False, visible,
            )
            return carry

        lax.fori_loop(0, lax.div(count_ref[0, member] + BLOCK_PAGES - 1, BLOCK_PAGES), one_block, 0)

    over_groups(old_keys)

    if closing:
        for member in range(per_node):

            def one_out(head, carry, member=member):
                place = member * heads + head
                result = acc_ref[place] * (1.0 / total_ref[place])
                out_ref[member, :, pl.ds(pl.multiple_of(head * HD, HD), HD)] = result.astype(out_ref.dtype).T
                return carry

            lax.fori_loop(0, heads, one_out, 0, unroll=2)


def attend(nodes, capacity, page_pool_dtype, page_shape, most_pages, tables, queries, stage, inputs, opening, closing):
    per_node, suffix, query_width = queries.shape
    page_len = page_shape[1]
    heads = query_width // HD
    state_shape = [
        jax.ShapeDtypeStruct((per_node * heads, HD, suffix), jnp.float32),
        jax.ShapeDtypeStruct((per_node * heads, 1, suffix), jnp.float32),
        jax.ShapeDtypeStruct((per_node * heads, 1, suffix), jnp.float32),
    ]

    slots = capacity if opening else sum(last - first for _, first, last in stage)
    slots = -(-min(slots, most_pages) // BLOCK_PAGES) * BLOCK_PAGES
    in_specs = [VMEM] + ([VMEM, ANY] if opening else [VMEM] * 3 + [ANY] * len(stage))
    out_specs = [VMEM] * (4 if closing else 3)
    result_shape = ([jax.ShapeDtypeStruct(queries.shape, queries.dtype)] if closing else []) + state_shape
    scratch = [
        pltpu.VMEM((per_node, slots) + page_shape, page_pool_dtype),
        pltpu.VMEM((2, BLOCK_PAGES * page_len, suffix), jnp.float32),
        pltpu.VMEM((2, BLOCK_PAGES * page_len, suffix), page_pool_dtype),
        pltpu.SMEM((nodes,), jnp.int32),
        pltpu.SMEM((2, per_node), jnp.int32),
        pltpu.SemaphoreType.DMA((per_node, slots)),
    ]
    if closing:
        out_specs = [VMEM]
        result_shape = result_shape[:1]
        scratch = [pltpu.VMEM(s.shape, s.dtype) for s in state_shape] + scratch
    work = (slots + (per_node * 2 if opening else 0)) * page_len * heads * suffix
    return pl.pallas_call(
        functools.partial(
            attend_kernel, nodes, per_node, most_pages, page_len, stage, opening, closing
        ),
        grid_spec=pltpu.PrefetchScalarGridSpec(
            num_scalar_prefetch=5, grid=(), in_specs=in_specs, out_specs=out_specs, scratch_shapes=scratch
        ),
        out_shape=result_shape,
        compiler_params=pltpu.CompilerParams(vmem_limit_bytes=40 * 1024 * 1024),
        cost_estimate=pl.CostEstimate(
            flops=work * 4 * HD * 2, bytes_accessed=12 * 1024 * 1024, transcendentals=work
        ),
        name="attend",
    )(*tables, queries, *inputs)


def body(queries, new_kv, page_pool, slot_request, prefix_len, page_holder, page_slot, decode_slot):
    nodes = lax.axis_size("node")
    me = lax.axis_index("node").astype(jnp.int32).reshape(1)
    per_node, suffix, query_width = queries.shape
    page_len, width = page_pool.shape[2:]
    most_pages = page_holder.shape[1]
    capacity = page_pool.shape[1] // nodes
    stages = message_plan(nodes, capacity)
    messages = [message for stage in stages for message in stage]
    tables = (slot_request, prefix_len, page_holder, page_slot, me)
    page_shape = (2, page_len, width)
    packed = pl.pallas_call(
        functools.partial(pack_kernel, nodes, per_node, most_pages, page_len, messages),
        grid_spec=pltpu.PrefetchScalarGridSpec(
            num_scalar_prefetch=5,
            grid=(),
            in_specs=[ANY, ANY, pl.BlockSpec(memory_space=pltpu.SMEM)],
            out_specs=[VMEM] * (len(messages) + nodes - 1) + [pl.BlockSpec(memory_space=pltpu.SMEM)],
            scratch_shapes=[
                pltpu.SemaphoreType.DMA((max(nodes - 1, 1), capacity)),
                pltpu.SemaphoreType.DMA((max(nodes - 1, 1),)),
            ],
        ),
        out_shape=[jax.ShapeDtypeStruct((last - first,) + page_shape, page_pool.dtype) for _, first, last in messages]
        + [jax.ShapeDtypeStruct((2, suffix, width), new_kv.dtype)] * (nodes - 1)
        + [jax.ShapeDtypeStruct((2 * per_node,), jnp.int32)],
        name="pack",
    )(*tables, page_pool, new_kv, decode_slot)

    waiting = dict(zip(messages, packed))
    handing, sources = packed[len(messages) : -1], packed[-1]
    attending = functools.partial(
        attend, nodes, capacity, page_pool.dtype, page_shape, most_pages, tables, queries
    )

    def shifted(array, k):
        return lax.ppermute(array, "node", [(i, (i + k) % nodes) for i in range(nodes)])

    def send_after(earlier, array, k):
        if earlier is not None:
            arrived[earlier], array = lax.optimization_barrier((arrived[earlier], array))
        return shifted(array, k)

    arrived, latest, handed = {}, {}, {}
    for stage in stages:
        for message in stage:
            k = message[0]
            arrived[message] = send_after(latest.get(k), waiting[message], k)
            latest[k] = message
    for k in latest:
        handed[k] = send_after(latest[k], handing[k - 1], k)

    state = attending([], [new_kv, page_pool], True, not stages)
    for index, stage in enumerate(stages):
        inputs = list(state) + [arrived[message] for message in stage]
        state = attending(stage, inputs, False, index == len(stages) - 1)
    slots = []
    for slot in range(per_node):
        shift, member = sources[2 * slot], sources[2 * slot + 1]
        chosen = new_kv[:, 0]
        for other in range(1, per_node):
            chosen = jnp.where(member == other, new_kv[:, other], chosen)
        for k in range(1, nodes):
            chosen = jnp.where(shift == k, handed[k], chosen)
        slots.append(chosen)
    return state[0], jnp.stack(slots, axis=1)


def solution(mesh):
    placed = (
        P(("groups", "node"), None, "tp"),
        P(None, ("groups", "node"), None, "tp"),
        P(None, ("groups", "node"), None, "tp"),
        P("groups"),
        P("groups"),
        P("groups", None),
        P("groups", None),
        P("groups"),
    )
    return jax.shard_map(
        body,
        mesh=mesh,
        in_specs=placed,
        out_specs=(P(("groups", "node"), None, "tp"), P(None, ("groups", "node"), None, "tp")),
        check_vma=False,
    )
```

```python
import functools
import math

import jax
import jax.numpy as jnp
from jax import lax
from jax.experimental import pallas as pl
from jax.experimental.pallas import tpu as pltpu
from jax.sharding import PartitionSpec as P

HD = 128
OWN_BLOCK_PAGES = 4
BLOCK_PAGES = 6
MASKED = -1e30
ANY = pl.BlockSpec(memory_space=pl.ANY)
VMEM = pl.BlockSpec(memory_space=pltpu.VMEM)


def message_plan(nodes, capacity):
    half = nodes // 2
    shifts = [half] * (nodes > 1) + [k for k in range(1, nodes) if k != half]
    cut = (capacity + 1) // 2
    stages = [[(k, 0, cut) for k in shifts]] if shifts else []
    if cut < capacity and shifts:
        stages.append([(k, cut, capacity) for k in shifts])
    return stages


def pages_of(prefix_len_ref, request, page_len):
    return lax.div(prefix_len_ref[request] + page_len - 1, page_len)


def pack_kernel(
    nodes, per_node, most_pages, page_len, messages,
    request_ref, len_ref, holder_ref, slot_ref, node_ref, pool_ref, new_ref, decode_ref,
    *rest,
):
    page_out = rest[: len(messages)]
    decode_out = rest[len(messages) : len(messages) + nodes - 1]
    source_ref, page_sem, decode_sem = rest[len(messages) + nodes - 1 :]
    me = node_ref[0]

    def page_copy(index, offset, slot):
        k, first, _ = messages[index]
        return pltpu.make_async_copy(
            pool_ref.at[:, slot], page_out[index].at[offset], page_sem.at[k - 1, first + offset]
        )

    counts = []
    for k in range(1, nodes):
        there = lax.rem(me + k, nodes)
        arrival = jnp.int32(0)
        for member in range(per_node):
            request = request_ref[there * per_node + member]
            page_total = pages_of(len_ref, request, page_len)

            def one_page(j, arrival, k=k, request=request):
                here = holder_ref[request, j] == me

                @pl.when(here)
                def _():
                    slot = slot_ref[request, j]
                    for index, (shift, first, last) in enumerate(messages):
                        if shift == k:

                            @pl.when((arrival >= first) & (arrival < last))
                            def _():
                                page_copy(index, arrival - first, slot).start()

                return arrival + here.astype(jnp.int32)

            arrival = lax.fori_loop(0, page_total, one_page, arrival)
        counts.append(arrival)

    def decode_copies(act):
        for k in range(1, nodes):
            there = lax.rem(me + k, nodes)
            for member in range(per_node):
                target = decode_ref[request_ref[me * per_node + member]]

                @pl.when(lax.div(target, per_node) == there)
                def _():
                    act(
                        pltpu.make_async_copy(
                            new_ref.at[:, member], decode_out[k - 1], decode_sem.at[k - 1]
                        )
                    )

    decode_copies(lambda copy: copy.start())

    def one_source(p, carry):
        wanted = decode_ref[request_ref[p]] - me * per_node

        @pl.when((wanted >= 0) & (wanted < per_node))
        def _():
            source_ref[2 * wanted] = lax.rem(me - lax.div(p, per_node) + nodes, nodes)
            source_ref[2 * wanted + 1] = lax.rem(p, per_node)

        return carry

    lax.fori_loop(0, nodes * per_node, one_source, 0)

    for index, (k, first, last) in enumerate(messages):
        for offset in range(last - first):

            @pl.when(first + offset < counts[k - 1])
            def _():
                page_copy(index, offset, 0).wait()

    decode_copies(lambda copy: copy.wait())


def head_pipeline(count, scores_of, place_of, top_ref, total_ref, acc_ref, score_ref, weight_ref, turned, rate, fresh, visible):
    def soften(h):
        place = place_of(h)
        scores = visible(score_ref[h % 2])
        top = jnp.max(scores, axis=0, keepdims=True)
        if not fresh:
            before = top_ref[place]
            top = jnp.maximum(before, top)
            fade = jnp.exp2((before - top) * rate)
            fade_of[h] = fade
        weights = jnp.exp2((scores - top) * rate)
        total = jnp.sum(weights, axis=0, keepdims=True)
        top_ref[place] = top
        total_ref[place] = total if fresh else total_ref[place] * fade + total
        weight_ref[h % 2] = weights.astype(weight_ref.dtype)

    def gather(h):
        place = place_of(h)
        product = jnp.dot(turned, weight_ref[h % 2], preferred_element_type=jnp.float32)
        acc_ref[place] = product if fresh else acc_ref[place] * fade_of[h] + product

    fade_of = {}
    for step in range(count + 2):
        if step < count:
            score_ref[step % 2] = scores_of(step)
        if 0 <= step - 2 < count:
            gather(step - 2)
        if 0 <= step - 1 < count:
            soften(step - 1)


def attend_kernel(
    nodes, per_node, most_pages, page_len, messages, opening, closing,
    request_ref, len_ref, holder_ref, slot_ref, node_ref, query_ref, *rest,
):
    if opening:
        new_ref, pool_ref = rest[:2]
        rest = rest[2:]
    else:
        old_acc, old_top, old_total = rest[:3]
        received = rest[3 : 3 + len(messages)]
        rest = rest[3 + len(messages) :]
    if closing:
        out_ref, acc_ref, top_ref, total_ref = rest[:4]
        rest = rest[4:]
    else:
        acc_ref, top_ref, total_ref = rest[:3]
        rest = rest[3:]
    page_ref, score_ref, weight_ref, arrival_ref, count_ref, page_sem = rest
    me = node_ref[0]
    width = page_ref.shape[-1]
    groups = width // HD
    per_group = query_ref.shape[2] // width
    heads = groups * per_group
    suffix = query_ref.shape[1]
    block_pages = score_ref.shape[1] // page_len
    block_keys = block_pages * page_len
    rate = HD ** (-0.5) * math.log2(math.e)

    for holder in range(nodes):
        arrival_ref[holder] = 0
    for member in range(per_node):
        request = request_ref[me * per_node + member]

        def one_page(j, carry, request=request, member=member):
            count, keys = carry
            holder = holder_ref[request, j]
            arrival = arrival_ref[holder]
            arrival_ref[holder] = arrival + 1
            shift = lax.rem(me - holder + nodes, nodes)
            sem = page_sem.at[member, count]
            place = page_ref.at[member, count]
            if opening:
                taken = shift == 0

                @pl.when(taken)
                def _():
                    pltpu.make_async_copy(pool_ref.at[:, slot_ref[request, j]], place, sem).start()

            else:
                taken = jnp.bool_(False)
                for index, (k, first, last) in enumerate(messages):
                    match = (shift == k) & (arrival >= first) & (arrival < last)
                    taken = taken | match

                    @pl.when(match)
                    def _():
                        pltpu.make_async_copy(received[index].at[arrival - first], place, sem).start()

            filled = jnp.minimum(len_ref[request] - j * page_len, page_len)
            return (
                count + taken.astype(jnp.int32),
                keys + jnp.where(taken, filled, 0),
            )

        count, keys = lax.fori_loop(
            0, pages_of(len_ref, request, page_len), one_page, (jnp.int32(0), jnp.int32(0))
        )
        count_ref[0, member] = count
        count_ref[1, member] = keys

    def head_lanes(group, h):
        return pl.ds(pl.multiple_of((group * per_group + h) * HD, HD), HD)

    def over_groups(act):
        def one_group(i, carry):
            member, group = lax.div(i, groups), lax.rem(i, groups)
            act(member, group, pl.ds(pl.multiple_of(group * HD, HD), HD))
            return carry

        lax.fori_loop(0, per_node * groups, one_group, 0)

    if opening:
        row = lax.broadcasted_iota(jnp.int32, (suffix, suffix), 0)
        column = lax.broadcasted_iota(jnp.int32, (suffix, suffix), 1)

        def new_keys(member, group, lanes):
            keys_new = new_ref[0, member, :, lanes]
            values_new = new_ref[1, member, :, lanes].T

            def scores_of(h):
                query = query_ref[member, :, head_lanes(group, h)]
                return lax.dot_general(
                    keys_new, query, (((1,), (1,)), ((), ())), preferred_element_type=jnp.float32
                )

            head_pipeline(
                per_group, scores_of, lambda h: member * heads + group * per_group + h,
                top_ref, total_ref, acc_ref, score_ref.at[:, :suffix], weight_ref.at[:, :suffix], values_new, rate, True,
                lambda scores: jnp.where(row <= column, scores, MASKED),
            )

        over_groups(new_keys)
    else:
        acc_ref[...] = old_acc[...]
        top_ref[...] = old_top[...]
        total_ref[...] = old_total[...]

    def wait_member(member, carry):
        def wait_page(i, carry):
            pltpu.make_async_copy(page_ref.at[member, i], page_ref.at[member, i], page_sem.at[member, i]).wait()
            return carry

        return lax.fori_loop(0, count_ref[0, member], wait_page, carry)

    lax.fori_loop(0, per_node, wait_member, 0)

    def old_keys(member, group, lanes):
        def one_block(b, carry):
            pages = pl.ds(b * block_pages, block_pages)
            valid = count_ref[1, member] - b * block_keys

            block_key = page_ref[member, pages, 0, :, lanes].reshape(block_keys, HD)
            block_values = page_ref[member, pages, 1, :, lanes].reshape(block_keys, HD)
            row = lax.broadcasted_iota(jnp.int32, (block_keys, HD), 0)
            block_values = jnp.where(row < valid, block_values, jnp.zeros_like(block_values))

            def scores_of(h):
                query = query_ref[member, :, head_lanes(group, h)]
                return lax.dot_general(
                    block_key, query, (((1,), (1,)), ((), ())), preferred_element_type=jnp.float32
                )

            def visible(scores):
                row = lax.broadcasted_iota(jnp.int32, scores.shape, 0)
                return jnp.where(row < valid, scores, MASKED)

            head_pipeline(
                per_group, scores_of, lambda h: member * heads + group * per_group + h,
                top_ref, total_ref, acc_ref, score_ref, weight_ref, block_values.T, rate, False, visible,
            )
            return carry

        lax.fori_loop(0, lax.div(count_ref[0, member] + block_pages - 1, block_pages), one_block, 0)

    over_groups(old_keys)

    if closing:
        for member in range(per_node):

            def one_out(head, carry, member=member):
                place = member * heads + head
                result = acc_ref[place] * (1.0 / total_ref[place])
                out_ref[member, :, pl.ds(pl.multiple_of(head * HD, HD), HD)] = result.astype(out_ref.dtype).T
                return carry

            lax.fori_loop(0, heads, one_out, 0, unroll=2)


def attend(nodes, capacity, page_pool_dtype, page_shape, most_pages, tables, queries, stage, inputs, opening, closing):
    per_node, suffix, query_width = queries.shape
    page_len = page_shape[1]
    heads = query_width // HD
    state_shape = [
        jax.ShapeDtypeStruct((per_node * heads, HD, suffix), jnp.float32),
        jax.ShapeDtypeStruct((per_node * heads, 1, suffix), jnp.float32),
        jax.ShapeDtypeStruct((per_node * heads, 1, suffix), jnp.float32),
    ]

    slots = capacity if opening else sum(last - first for _, first, last in stage)
    block_pages = OWN_BLOCK_PAGES if opening else BLOCK_PAGES
    slots = -(-min(slots, most_pages) // block_pages) * block_pages
    in_specs = [VMEM] + ([VMEM, ANY] if opening else [VMEM] * 3 + [ANY] * len(stage))
    out_specs = [VMEM] * (4 if closing else 3)
    result_shape = ([jax.ShapeDtypeStruct(queries.shape, queries.dtype)] if closing else []) + state_shape
    scratch = [
        pltpu.VMEM((per_node, slots) + page_shape, page_pool_dtype),
        pltpu.VMEM((2, block_pages * page_len, suffix), jnp.float32),
        pltpu.VMEM((2, block_pages * page_len, suffix), page_pool_dtype),
        pltpu.SMEM((nodes,), jnp.int32),
        pltpu.SMEM((2, per_node), jnp.int32),
        pltpu.SemaphoreType.DMA((per_node, slots)),
    ]
    if closing:
        out_specs = [VMEM]
        result_shape = result_shape[:1]
        scratch = [pltpu.VMEM(s.shape, s.dtype) for s in state_shape] + scratch
    work = (slots + (per_node * 2 if opening else 0)) * page_len * heads * suffix
    return pl.pallas_call(
        functools.partial(
            attend_kernel, nodes, per_node, most_pages, page_len, stage, opening, closing
        ),
        grid_spec=pltpu.PrefetchScalarGridSpec(
            num_scalar_prefetch=5, grid=(), in_specs=in_specs, out_specs=out_specs, scratch_shapes=scratch
        ),
        out_shape=result_shape,
        compiler_params=pltpu.CompilerParams(vmem_limit_bytes=40 * 1024 * 1024),
        cost_estimate=pl.CostEstimate(
            flops=work * 4 * HD * 2, bytes_accessed=12 * 1024 * 1024, transcendentals=work
        ),
        name="attend",
    )(*tables, queries, *inputs)


def body(queries, new_kv, page_pool, slot_request, prefix_len, page_holder, page_slot, decode_slot):
    nodes = lax.axis_size("node")
    me = lax.axis_index("node").astype(jnp.int32).reshape(1)
    per_node, suffix, query_width = queries.shape
    page_len, width = page_pool.shape[2:]
    most_pages = page_holder.shape[1]
    capacity = page_pool.shape[1] // nodes
    stages = message_plan(nodes, capacity)
    messages = [message for stage in stages for message in stage]
    tables = (slot_request, prefix_len, page_holder, page_slot, me)
    page_shape = (2, page_len, width)
    packed = pl.pallas_call(
        functools.partial(pack_kernel, nodes, per_node, most_pages, page_len, messages),
        grid_spec=pltpu.PrefetchScalarGridSpec(
            num_scalar_prefetch=5,
            grid=(),
            in_specs=[ANY, ANY, pl.BlockSpec(memory_space=pltpu.SMEM)],
            out_specs=[VMEM] * (len(messages) + nodes - 1) + [pl.BlockSpec(memory_space=pltpu.SMEM)],
            scratch_shapes=[
                pltpu.SemaphoreType.DMA((max(nodes - 1, 1), capacity)),
                pltpu.SemaphoreType.DMA((max(nodes - 1, 1),)),
            ],
        ),
        out_shape=[jax.ShapeDtypeStruct((last - first,) + page_shape, page_pool.dtype) for _, first, last in messages]
        + [jax.ShapeDtypeStruct((2, suffix, width), new_kv.dtype)] * (nodes - 1)
        + [jax.ShapeDtypeStruct((2 * per_node,), jnp.int32)],
        name="pack",
    )(*tables, page_pool, new_kv, decode_slot)

    waiting = dict(zip(messages, packed))
    handing, sources = packed[len(messages) : -1], packed[-1]
    attending = functools.partial(
        attend, nodes, capacity, page_pool.dtype, page_shape, most_pages, tables, queries
    )

    def shifted(array, k):
        return lax.ppermute(array, "node", [(i, (i + k) % nodes) for i in range(nodes)])

    def send_after(earlier, array, k):
        if earlier is not None:
            arrived[earlier], array = lax.optimization_barrier((arrived[earlier], array))
        return shifted(array, k)

    arrived, latest, handed = {}, {}, {}
    for stage in stages:
        for message in stage:
            k = message[0]
            arrived[message] = send_after(latest.get(k), waiting[message], k)
            latest[k] = message
    for k in latest:
        handed[k] = send_after(latest[k], handing[k - 1], k)

    state = attending([], [new_kv, page_pool], True, not stages)
    for index, stage in enumerate(stages):
        inputs = list(state) + [arrived[message] for message in stage]
        state = attending(stage, inputs, False, index == len(stages) - 1)
    slots = []
    for slot in range(per_node):
        shift, member = sources[2 * slot], sources[2 * slot + 1]
        chosen = new_kv[:, 0]
        for other in range(1, per_node):
            chosen = jnp.where(member == other, new_kv[:, other], chosen)
        for k in range(1, nodes):
            chosen = jnp.where(shift == k, handed[k], chosen)
        slots.append(chosen)
    return state[0], jnp.stack(slots, axis=1)


def solution(mesh):
    placed = (
        P(("groups", "node"), None, "tp"),
        P(None, ("groups", "node"), None, "tp"),
        P(None, ("groups", "node"), None, "tp"),
        P("groups"),
        P("groups"),
        P("groups", None),
        P("groups", None),
        P("groups"),
    )
    return jax.shard_map(
        body,
        mesh=mesh,
        in_specs=placed,
        out_specs=(P(("groups", "node"), None, "tp"), P(None, ("groups", "node"), None, "tp")),
        check_vma=False,
    )
```
